512 devices in a mesh: row: 64 (over y, z), col: 8 (over x, core).
Axes of the slice: x: 4, y: 8, z: 8, core: 2. Of those that a mesh axis runs over, the one named last changes fastest.
Arguments:
- a_tiles: bfloat16 [1024, 7, 4096], P('row'), may hold values from -0.25 to 0.25
- neighbors: int32 [1024, 7], P('row'), may hold values from 0 to 527, as said below
- send_rows: int32 [64, 512], P('row'), may hold values from 0 to 15
- p_tiles: bfloat16 [1024, 8, 4096], P('row', 'col'), may hold values from -0.5 to 0.5
- p_index: int32 [1024, 8], P('row', 'col'), may hold values from 0 to 1
Outputs:
- coarse: float32 [1024, 1024], P('row', 'col')
The draws below stay inside these ranges and needn't reach their ends.
Inputs may be any that keep to these rules, and one draw needn't show every extreme that they name: `neighbors`: column 0 of a row names the row itself (local index). Other entries below 16 are local rows. An entry v >= 16 names slot s = (v - 16) % 8 filled by device p = (v - 16) // 8, never the reading device itself; s < 8 when p is next to the reader along the row axis (with wrap), s < 4 otherwise.
All inputs are finite; a program needn't handle non-finite values.
Results may differ from the reference program's by a relative error of at most 0.0029.
Values may be sent and summed in bfloat16 or wider, within the bound.
A program may use at most 64 MiB of HBM per device.

```python
import jax
import jax.numpy as jnp
from jax import lax

B = 64
K = 7
CP = 2
S = 8
S2 = 4
R_DEV = 16
NF = 1024
N_ROW = 64
N_COL = 8


def ghost_counts(key):
    far_key = jax.random.fold_in(key, 11)
    source = jnp.arange(N_ROW)[:, None]
    target = jnp.arange(N_ROW)[None, :]
    gap = (target - source) % N_ROW
    far = jax.random.randint(far_key, (N_ROW, N_ROW), max(S2 - 1, 1), S2 + 1)
    near = (gap == 1) | (gap == N_ROW - 1)
    counts = jnp.where(near, S, jnp.where(gap == 2, S2, jnp.where(gap == 0, 0, far)))
    return counts.astype(jnp.int32)


def draw_neighbors(key, part):
    counts = ghost_counts(key)
    pick_key = jax.random.fold_in(key, 37)
    slots = jnp.arange(S, dtype=jnp.int32)
    sources = jnp.arange(N_ROW, dtype=jnp.int32)
    total_codes = N_ROW * S

    def for_device(target):
        gap = (target - sources) % N_ROW
        live = slots[None, :] < counts[:, target][:, None]
        forced = (gap == 1) | (gap == N_ROW - 1) | (gap == 2) | (gap == N_ROW // 2)
        code = R_DEV + sources[:, None] * S + slots[None, :]
        rank = jax.random.permutation(jax.random.fold_in(pick_key, target), total_codes).astype(jnp.int32).reshape(N_ROW, S)
        score = jnp.where(live & forced[:, None], rank, jnp.where(live, rank + total_codes, rank + 2 * total_codes))
        order = jnp.argsort(score.reshape(-1), stable=True)
        total = jnp.sum(live.astype(jnp.int32))
        pick = jnp.arange(R_DEV * 4, dtype=jnp.int32) % total
        return code.reshape(-1)[order[pick]].reshape(R_DEV, 4)
    remote = jax.vmap(for_device)(sources).reshape(N_ROW * R_DEV, 4)
    local_key = jax.random.fold_in(key, 23)
    local = jax.random.randint(local_key, (N_ROW * R_DEV, K - 5), 0, R_DEV)
    itself = (jnp.arange(N_ROW * R_DEV, dtype=jnp.int32) % R_DEV)[:, None]
    return jnp.concatenate([itself, remote, local], axis=1).astype(jnp.int32)


def set_ends(values, stream_key, low, largest):
    longest = values.shape.index(max(values.shape))
    spots = []
    for shift in (0, 1):
        where = [jax.random.randint(jax.random.fold_in(stream_key, axis), (), 0, length) for axis, length in enumerate(values.shape)]
        where[longest] = (where[longest] + shift) % values.shape[longest]
        spots.append(tuple(where))
    return values.at[spots[0]].set(low).at[spots[1]].set(largest)


def block_levels(rng, shape, pieces, least, high):
    level = 1.0
    for dim, parts in pieces:
        heights = jax.random.uniform(jax.random.fold_in(jax.random.fold_in(rng, 6), dim), (parts,), jnp.float32, least / len(pieces), high / len(pieces))
        level = level * jnp.repeat(jnp.exp(heights), shape[dim] // parts).reshape((-1,) + (1,) * (len(shape) - 1 - dim))
    return level


def normal_values(stream_key, shape, deviation, limit, split=(), kind=jnp.bfloat16):
    level = block_levels(stream_key, shape, split, -0.22, 0.18) if split else 1.0
    values = jax.random.normal(stream_key, shape, jnp.float32) * deviation * level
    return jnp.minimum(jnp.maximum(values, -limit), limit).astype(kind)


def setup_inputs(seed: int = 0) -> dict:
    key_of = jax.random.split(jax.random.key(seed), 6)
    a_tiles = normal_values(key_of[0], (NF, K, B * B), (K * B) ** -0.5, 0.25, ((0, 64),))
    neighbors = draw_neighbors(jax.random.fold_in(key_of[5], 71), 0)
    send_rows = set_ends(jax.random.randint(key_of[2], (N_ROW, N_ROW * S), 0, R_DEV), jax.random.fold_in(key_of[2], 1), 0, R_DEV - 1).astype(jnp.int32)
    p_tiles = normal_values(key_of[3], (NF, N_COL, B * B), ((R_DEV * N_ROW * B // (2 * CP)) ** 0.5) ** -0.5, 0.5, ((0, 64), (1, 8)))
    p_index = set_ends(jax.random.randint(key_of[4], (NF, N_COL), 0, CP), jax.random.fold_in(key_of[4], 1), 0, CP - 1).astype(jnp.int32)
    return {"a_tiles": a_tiles, "neighbors": neighbors, "send_rows": send_rows, "p_tiles": p_tiles, "p_index": p_index}


def reference(a_tiles, neighbors, send_rows, p_tiles, p_index):
    panels = p_tiles.shape[1]
    flat_send = send_rows.reshape(-1)
    coarse_blocks = CP * panels

    def device_term(q, total):
        code = lax.dynamic_slice_in_dim(neighbors, q * R_DEV, R_DEV, 0)
        local = code < R_DEV
        ghost = jnp.maximum(code - R_DEV, 0)
        source = ghost // S
        slot = ghost % S
        remote = source * R_DEV + flat_send[source * (N_ROW * S) + q * S + slot]
        glob = jnp.where(local, q * R_DEV + code, remote).astype(jnp.int32)
        tiles = p_tiles[glob].astype(jnp.float32).reshape(R_DEV, K, panels, B, B)
        index = p_index[glob]
        hit = (index[..., None] == jnp.arange(CP)[None, None, None, :]).astype(jnp.float32)
        block_rows = lax.dynamic_slice_in_dim(a_tiles, q * R_DEV, R_DEV, 0)
        coupling = block_rows.astype(jnp.float32).reshape(R_DEV, K, B, B)
        inner = jnp.einsum('rkij,rkcjl->rkcil', coupling, tiles, precision=lax.Precision.HIGHEST)
        product = jnp.einsum('rkcil,rkcb->ricbl', inner, hit, precision=lax.Precision.HIGHEST)
        product = product.astype(jnp.bfloat16).astype(jnp.float32).reshape(R_DEV * B, coarse_blocks * B)
        mine = lax.dynamic_slice_in_dim(p_tiles, q * R_DEV, R_DEV, 0).astype(jnp.float32).reshape(R_DEV, panels, B, B)
        mine_index = lax.dynamic_slice_in_dim(p_index, q * R_DEV, R_DEV, 0)
        mine_hit = (mine_index[..., None] == jnp.arange(CP)[None, None, :]).astype(jnp.float32)
        dense = jnp.einsum('rcix,rcy->ricyx', mine, mine_hit, precision=lax.Precision.HIGHEST)
        dense = dense.reshape(R_DEV * B, coarse_blocks * B)
        return total + jnp.dot(dense.T, product, precision=lax.Precision.HIGHEST, preferred_element_type=jnp.float32)

    start = jnp.zeros((coarse_blocks * B, coarse_blocks * B), jnp.float32)
    return lax.fori_loop(0, N_ROW, device_term, start)
```

```python
import functools

import jax
import jax.numpy as jnp
from jax import lax
from jax.experimental import pallas as pl
from jax.experimental.pallas import tpu as pltpu
from jax.sharding import PartitionSpec as P

MESH = pl.DeviceIdType.MESH
LINE = 8
R = 16
K = 7
GROUPS = R * K // 8
F32, BF16, I32 = jnp.float32, jnp.bfloat16, jnp.int32
META1, SPREAD_Y, SPREAD_Z, PANEL, PINDEX, META2, FWD_Y, FWD_Z, REQ_Y, REQ_Z, GHOST_Y, GHOST_Z, SUM_Y, SUM_Z, LAST_Y, LAST_Z = range(16)


def iota(shape, dim):
    return lax.broadcasted_iota(I32, shape, dim)


def kernel(
    p_ref, p2_ref, a_ref, meta_ref, want_ref, idx_ref, out_ref,
    store_y, store_z, meta_y, meta_all, table, request, req_y, req_z,
    pack_y, pack_z, ghost, panel, idx_all, pick, spread, terms, lhs, wide,
    ap, apb, partial, send_y, send_z, sum_y, sum_z, half_y, half_z, last_y, last_z,
    send_sem, recv_sem,
):
    row, c = lax.axis_index("row"), lax.axis_index("col")
    y, z = row // LINE, row % LINE
    place = {"y": y, "z": z, "c": c}

    def target(axis, t):
        if axis == "y":
            return (t * LINE + z, c)
        if axis == "z":
            return (y * LINE + t, c)
        return (row, t)

    def others(axis):
        return [(place[axis] + d) % LINE for d in range(1, LINE)]

    def copy(phase, axis, t, src, dst, mine):
        return pltpu.make_async_remote_copy(
            src_ref=src, dst_ref=dst, send_sem=send_sem.at[phase, t], recv_sem=recv_sem.at[phase, mine],
            device_id=target(axis, t), device_id_type=MESH,
        )

    started = []

    def push(phase, axis, src, dst):
        me = place[axis]
        for t in others(axis):
            op = copy(phase, axis, t, src(t), dst(me), me)
            op.start()
            started.append(op)

    def arrived(phase, axis, dst):
        for t in others(axis):
            copy(phase, axis, t, dst(t), dst(t), t).wait_recv()

    barrier = pltpu.get_barrier_semaphore()
    for axis in ("y", "z", "c"):
        for t in others(axis):
            pl.semaphore_signal(barrier, inc=1, device_id=target(axis, t), device_id_type=MESH)
    pl.semaphore_wait(barrier, 3 * (LINE - 1))

    def stripe(s):
        return pl.ds(pl.multiple_of(s * 256, 256), 256)

    def rows(start, count):
        return pl.ds(pl.multiple_of(start, count), count)

    push(META1, "y", lambda t: meta_ref.at[t], lambda s: meta_y.at[s])
    push(SPREAD_Y, "y", lambda t: p_ref.at[:, stripe(t)], lambda s: store_y.at[rows(z * 128 + s * R, R)])
    push(SPREAD_Z, "z", lambda t: p_ref.at[:, stripe(LINE + t)], lambda s: store_z.at[rows(y * 128 + s * R, R)])
    meta_y[y] = meta_ref[y]
    store_y[rows(z * 128 + y * R, R)] = p_ref[:, stripe(y)]
    store_z[rows(y * 128 + z * R, R)] = p_ref[:, stripe(LINE + z)]
    arrived(META1, "y", lambda s: meta_y.at[s])
    push(META2, "z", lambda t: meta_y, lambda s: meta_all.at[s])
    arrived(SPREAD_Y, "y", lambda s: store_y.at[rows(z * 128 + s * R, R)])
    push(FWD_Y, "z", lambda t: store_y.at[rows(z * 128, 128)], lambda s: store_y.at[rows(s * 128, 128)])
    arrived(SPREAD_Z, "z", lambda s: store_z.at[rows(y * 128 + s * R, R)])
    push(FWD_Z, "y", lambda t: store_z.at[rows(y * 128, 128)], lambda s: store_z.at[rows(s * 128, 128)])

    panel[c] = p2_ref[...].astype(F32).T.astype(BF16)
    idx_all[c] = idx_ref[...]
    push(PANEL, "c", lambda t: panel.at[c], lambda s: panel.at[s])
    push(PINDEX, "c", lambda t: idx_all.at[c], lambda s: idx_all.at[s])

    meta_all[z] = meta_y[...]
    arrived(META2, "z", lambda s: meta_all.at[s])
    for s in range(LINE):
        for t in range(LINE):
            table[pl.ds(t * LINE + s, 1), :] = meta_all[s, t]
    rows_of = table[...].astype(F32)
    source = iota((64, 128), 0)
    lane = iota((64, 128), 1)
    want = want_ref[...]
    remote = want - R
    total = jnp.zeros((64, 128), F32)
    for s in range(LINE):
        column = jnp.sum(jnp.where(lane == z * LINE + s, rows_of, 0.0), axis=1, keepdims=True)
        value = column + (source * R).astype(F32)
        total = total + jnp.where(source * LINE + s == remote, value, 0.0)
    fine = jnp.where(want < R, want + row * R, jnp.sum(total, axis=0, keepdims=True).astype(I32))
    request[...] = fine
    req_y[y] = fine
    req_z[z] = fine
    push(REQ_Y, "y", lambda t: request, lambda s: req_y.at[s])
    push(REQ_Z, "z", lambda t: request, lambda s: req_z.at[s])
    total = jnp.zeros((64, 128), F32)
    for t in range(R):
        total = total + jnp.where(source * R + t == fine, rows_of[:, 64 + t : 65 + t], 0.0)
    half_of = jnp.sum(total, axis=0, keepdims=True)

    def make_pick(n, _):
        r = iota((128, 1), 0)
        col = (r & 63)
        f = ((r >> 6) & 1) * 512 + (col & 1) * 256 + (col >> 2) * 16 + ((col >> 1) & 1) * 8 + n
        pick[rows(n * 128, 128), :] = jnp.where(iota((128, 1024), 1) == f, 1.0, 0.0).astype(BF16)
        return 0

    lax.fori_loop(0, 8, make_pick, 0)

    def make_spread(b, _):
        first = 8 * b // K
        for slot in range(8):
            j = 8 * b + slot
            i = j // K
            block = a_ref[(j % K) * R + i].astype(F32)
            low = jnp.where(i == first, 1.0, 0.0)
            spread[rows(b * 64, 32), slot * 128 : slot * 128 + 128] = (block * low).astype(BF16)
            spread[rows(b * 64 + 32, 32), slot * 128 : slot * 128 + 128] = (block * (1.0 - low)).astype(BF16)
        return 0

    lax.fori_loop(0, GROUPS, make_spread, 0)
    for n in range(4):
        terms[n] = jnp.dot(
            spread[...], pick[:, n * 256 : n * 256 + 256], preferred_element_type=F32
        ).astype(BF16)

    eye = iota((128, 128), 0) == iota((128, 128), 1)

    def serve(req, t, store, pack, swap):
        asked = req[t]
        column = jnp.sum(jnp.where(eye, asked, 0).astype(F32), axis=1, keepdims=True)[: GROUPS * 8].astype(I32)
        n = iota((1, 1024), 1)
        if swap:
            n = ((n >> 4) & 7) * 128 + (n >> 7) * R + (n & 15)
        hot = jnp.where(n == column, 1.0, 0.0).astype(BF16)
        got = jnp.dot(hot, store[...], preferred_element_type=F32)
        got = got.reshape(GROUPS, 8, 256)
        return jnp.concatenate([got[:, :, :128], got[:, :, 128:]], axis=1).astype(BF16)

    arrived(REQ_Y, "y", lambda s: req_y.at[s])
    arrived(FWD_Y, "z", lambda s: store_y.at[rows(s * 128, 128)])
    for t in others("y"):
        pack_y[t] = serve(req_y, t, store_y, pack_y, True)
        op = copy(GHOST_Y, "y", t, pack_y.at[t], ghost.at[:, rows(y * 16, 16), :], y)
        op.start()
        started.append(op)
    arrived(REQ_Z, "z", lambda s: req_z.at[s])
    arrived(FWD_Z, "y", lambda s: store_z.at[rows(s * 128, 128)])
    for t in others("z"):
        pack_z[t] = serve(req_z, t, store_z, pack_z, False)
        op = copy(GHOST_Z, "z", t, pack_z.at[t], ghost.at[:, rows(128 + z * 16, 16), :], z)
        op.start()
        started.append(op)
    ghost[:, rows(y * 16, 16), :] = serve(req_y, y, store_y, pack_y, True)
    ghost[:, rows(128 + z * 16, 16), :] = serve(req_z, z, store_z, pack_z, False)

    by_group = jnp.where(iota((GROUPS + 2, 128), 1) >> 3 == iota((GROUPS + 2, 128), 0), half_of, 0.0)
    by_slot = jnp.where((iota((128, 256), 0) & 7) == (iota((128, 256), 1) & 7), 1.0, 0.0)
    mask = jnp.dot(by_group.astype(BF16), by_slot.astype(BF16), preferred_element_type=F32)
    for b in range(GROUPS):
        upper = mask[b : b + 1]
        for h, m in ((0, 1.0 - upper), (1, upper)):
            for n in range(4):
                lhs[b, h * 256 + n * 64 : h * 256 + n * 64 + 64, :] = (
                    terms[n, b * 64 : b * 64 + 64, :] * m.astype(BF16)
                )
    arrived(PANEL, "c", lambda s: panel.at[s])
    arrived(PINDEX, "c", lambda s: idx_all.at[s])

    def make_wide(n, _):
        upper = idx_all[n].astype(F32)
        for h, m in ((0, 1.0 - upper), (1, upper)):
            for pr in range(2):
                wide[rows(n * 128 + h * 64, 64), pr * 512 : pr * 512 + 512] = (
                    panel[n, pr * 64 : pr * 64 + 64, :] * m.astype(BF16)
                )
        return 0

    lax.fori_loop(0, LINE, make_wide, 0)
    ap[...] = jnp.zeros_like(ap)

    arrived(GHOST_Y, "y", lambda s: ghost.at[:, rows(s * 16, 16), :])
    arrived(GHOST_Z, "z", lambda s: ghost.at[:, rows(128 + s * 16, 16), :])

    left = iota((64, 128), 1) < 64

    def multiply(b, _):
        out = jnp.dot(lhs[b], ghost[b], preferred_element_type=F32)
        start = pl.multiple_of((8 * b // K) * 32, 32)
        for pr in range(2):
            u0 = out[pr * 128 : pr * 128 + 64]
            u1 = out[pr * 128 + 64 : pr * 128 + 128]
            v0 = out[256 + pr * 128 : 256 + pr * 128 + 64]
            v1 = out[256 + pr * 128 + 64 : 256 + pr * 128 + 128]
            ap[pr, pl.ds(start, 64), :] += jnp.where(left, u0 + pltpu.roll(u1, 64, 1), pltpu.roll(v0, 64, 1) + v1)
        return 0

    lax.fori_loop(0, GROUPS, multiply, 0)
    for pr in range(2):
        apb[pr * 512 : pr * 512 + 512] = ap[pr].astype(BF16)

    def project(n, _):
        block = jnp.dot(wide[rows(n * 128, 128), :], apb[...], preferred_element_type=F32)
        partial[n] = block.reshape(LINE, 2, 8, 128)
        return 0

    lax.fori_loop(0, LINE, project, 0)
    for n in range(LINE):
        send_y[n] = partial[n, :, 0].reshape(64, 128).astype(BF16)
    push(SUM_Y, "y", lambda t: send_y.at[t], lambda s: sum_y.at[s])
    for n in range(LINE):
        send_z[n] = partial[:, n, 1].reshape(64, 128).astype(BF16)
    push(SUM_Z, "z", lambda t: send_z.at[t], lambda s: sum_z.at[s])
    arrived(SUM_Y, "y", lambda s: sum_y.at[s])
    acc = partial[y, :, 0].reshape(64, 128)
    for t in others("y"):
        acc = acc + sum_y[t].astype(F32)
    half_y[...] = acc.reshape(LINE, 8, 128)
    push(LAST_Y, "z", lambda t: half_y.at[t], lambda s: last_y.at[s])
    arrived(SUM_Z, "z", lambda s: sum_z.at[s])
    acc = partial[:, z, 1].reshape(64, 128)
    for t in others("z"):
        acc = acc + sum_z[t].astype(F32)
    half_z[...] = acc.reshape(LINE, 8, 128)
    push(LAST_Z, "y", lambda t: half_z.at[t], lambda s: last_z.at[s])
    arrived(LAST_Y, "z", lambda s: last_y.at[s])
    acc = half_y[z]
    for t in others("z"):
        acc = acc + last_y[t]
    out_ref[0:8] = acc
    arrived(LAST_Z, "y", lambda s: last_z.at[s])
    acc = half_z[y]
    for t in others("y"):
        acc = acc + last_z[t]
    out_ref[8:16] = acc
    for op in started:
        op.wait_send()


def shards(a_tiles, neighbors, send_rows, p_tiles, p_index):
    tiles = p_tiles.reshape(R, 4096)
    tall = tiles.reshape(R * 32, 128)
    blocks = a_tiles.transpose(1, 0, 2).reshape(K * R, 32, 128)
    meta = jnp.concatenate(
        [
            send_rows.reshape(LINE, 1, 64),
            jnp.broadcast_to(p_index.reshape(1, 1, R), (LINE, 1, R)),
            jnp.zeros((LINE, 1, 128 - 64 - R), I32),
        ],
        axis=2,
    )
    want = jnp.pad(neighbors.reshape(1, R * K), ((0, 0), (0, 128 - R * K)))
    index = jnp.repeat(p_index.reshape(1, R), 32, axis=1)
    vmem = pl.BlockSpec(memory_space=pltpu.VMEM)
    V = pltpu.VMEM
    return pl.pallas_call(
        kernel,
        out_shape=jax.ShapeDtypeStruct((R, 128), F32),
        in_specs=[vmem] * 6,
        out_specs=vmem,
        scratch_shapes=[
            V((1024, 256), BF16), V((1024, 256), BF16),
            V((LINE, 1, 128), I32), V((LINE, LINE, 1, 128), I32), V((64, 128), I32),
            V((1, 128), I32), V((LINE, 1, 128), I32), V((LINE, 1, 128), I32),
            V((LINE, GROUPS, 16, 128), BF16), V((LINE, GROUPS, 16, 128), BF16),
            V((GROUPS, 256, 128), BF16),
            V((LINE, 128, 512), BF16), V((LINE, 1, 512), I32),
            V((1024, 1024), BF16), V((GROUPS * 64, 1024), BF16), V((4, GROUPS * 64, 256), BF16),
            V((GROUPS, 512, 256), BF16), V((1024, 1024), BF16),
            V((2, 512, 128), F32), V((1024, 128), BF16), V((LINE, LINE, 2, 8, 128), F32),
            V((LINE, 64, 128), BF16), V((LINE, 64, 128), BF16),
            V((LINE, 64, 128), BF16), V((LINE, 64, 128), BF16),
            V((LINE, 8, 128), F32), V((LINE, 8, 128), F32),
            V((LINE, 8, 128), F32), V((LINE, 8, 128), F32),
            pltpu.SemaphoreType.DMA((16, LINE)), pltpu.SemaphoreType.DMA((16, LINE)),
        ],
        compiler_params=pltpu.CompilerParams(
            collective_id=0, has_side_effects=True, vmem_limit_bytes=48 * 2**20
        ),
    )(tiles, tall, blocks, meta, want, index)


def solution(mesh):
    in_specs = (
        P("row", None, None),
        P("row", None),
        P("row", None),
        P("row", "col", None),
        P("row", "col"),
    )
    return jax.shard_map(shards, mesh=mesh, in_specs=in_specs, out_specs=P("row", "col"), check_vma=False)
```

```python
import functools

import jax
import jax.numpy as jnp
from jax import lax
from jax.experimental import pallas as pl
from jax.experimental.pallas import tpu as pltpu
from jax.sharding import PartitionSpec as P

MESH = pl.DeviceIdType.MESH
LINE = 8
R = 16
K = 7
FAR = K - 1
ASKED = R * FAR
GROUPS = ASKED // 8
F32, BF16, I32 = jnp.float32, jnp.bfloat16, jnp.int32
META1, SPREAD_Y, SPREAD_Z, PANEL, PINDEX, META2, FWD_Y, FWD_Z, REQ_Y, REQ_Z, GHOST_Y, GHOST_Z, SUM_Y, SUM_Z, LAST_Y, LAST_Z, NEXT_Y, NEXT_Z = range(18)


def iota(shape, dim):
    return lax.broadcasted_iota(I32, shape, dim)


def kernel(
    p_ref, a_ref, near_ref, sends_ref, index_ref, out_ref,
    raw, meta, store_y, store_z, meta_y, meta_all, table, request, req_y, req_z, hot_y, hot_z,
    pack_y, pack_z, ghost, panel, idx_all, order, tall, natural, own, pick, spread, terms, lhs, wide,
    own_pick, own_spread, own_terms,
    ap, apb, partial, send_y, send_z, sum_y, sum_z, half_y, half_z, last_y, last_z,
    send_sem, recv_sem, local_sem,
):
    row, c = lax.axis_index("row"), lax.axis_index("col")
    y, z = row // LINE, row % LINE
    place = {"y": y, "z": z, "c": c}

    def target(axis, t):
        if axis == "y":
            return (t * LINE + z, c)
        if axis == "z":
            return (y * LINE + t, c)
        return (row, t)

    def others(axis):
        return [(place[axis] + d) % LINE for d in range(1, LINE)]

    def copy(phase, axis, t, src, dst, mine):
        return pltpu.make_async_remote_copy(
            src_ref=src, dst_ref=dst, send_sem=send_sem.at[phase, t], recv_sem=recv_sem.at[phase, mine],
            device_id=target(axis, t), device_id_type=MESH,
        )

    started = []

    def push(phase, axis, src, dst):
        me = place[axis]
        for t in others(axis):
            op = copy(phase, axis, t, src(t), dst(me), me)
            op.start()
            started.append(op)

    def arrived(phase, axis, dst):
        for t in others(axis):
            copy(phase, axis, t, dst(t), dst(t), t).wait_recv()

    barrier = pltpu.get_barrier_semaphore()
    for axis in ("y", "z", "c"):
        for t in others(axis):
            pl.semaphore_signal(barrier, inc=1, device_id=target(axis, t), device_id_type=MESH)
    load = pltpu.make_async_copy(a_ref, raw, local_sem)
    load.start()

    indices = index_ref[...].astype(F32)
    for t in range(LINE):
        meta[t, :, :128] = sends_ref[:, t // 2 * 128 : t // 2 * 128 + 128]
        meta[t, :, 128:] = jnp.zeros((1, 128), I32)
        meta[t, :, 128 : 128 + R] = index_ref[...]
    couple = near_ref[...]
    to_lane = jnp.where(
        (iota((R, FAR * 128), 1) & 127) == iota((R, FAR * 128), 0) * FAR + (iota((R, FAR * 128), 1) >> 7), 1.0, 0.0
    ).astype(BF16)
    high = jnp.dot((couple >> 4).astype(F32).astype(BF16), to_lane, preferred_element_type=F32)
    low = jnp.dot((couple & 15).astype(F32).astype(BF16), to_lane, preferred_element_type=F32)
    want = jnp.zeros((1, 128), F32)
    for k in range(FAR):
        at = slice(k * 128, k * 128 + 128)
        want = want + high[k + 1 : k + 2, at] * 16.0 + low[k + 1 : k + 2, at]
    want = want.astype(I32)
    widen = jnp.where(iota((R, 512), 1) >> 5 == iota((R, 512), 0), 1.0, 0.0).astype(BF16)
    idx_all[c] = jnp.dot(
        jnp.broadcast_to(indices, (8, R)).astype(BF16), widen, preferred_element_type=F32
    )[:1]
    r = iota((512, 1), 0)
    order[...] = jnp.where(iota((512, 512), 1) == (r & 31) * R + (r >> 5), 1.0, 0.0).astype(BF16)
    for w in range(32):
        tall[w * R : w * R + R, K * 128 :] = p_ref[:, w * 128 : w * 128 + 128]
    own[...] = jnp.dot(order[...], tall[:, K * 128 :], preferred_element_type=F32).astype(BF16)
    panel[c] = own[...].astype(F32).T.astype(BF16)
    pl.semaphore_wait(barrier, 3 * (LINE - 1))

    def stripe(s):
        return pl.ds(pl.multiple_of(s * 256, 256), 256)

    def rows(start, count):
        return pl.ds(pl.multiple_of(start, count), count)

    push(META1, "y", lambda t: meta.at[t], lambda s: meta_y.at[s])
    push(SPREAD_Y, "y", lambda t: p_ref.at[:, stripe(t)], lambda s: store_y.at[rows(z * 128 + s * R, R)])
    push(SPREAD_Z, "z", lambda t: p_ref.at[:, stripe(LINE + t)], lambda s: store_z.at[rows(y * 128 + s * R, R)])
    push(PINDEX, "c", lambda t: idx_all.at[c], lambda s: idx_all.at[s])
    push(PANEL, "c", lambda t: panel.at[c], lambda s: panel.at[s])
    meta_y[y] = meta[y]
    store_y[rows(z * 128 + y * R, R)] = p_ref[:, stripe(y)]
    store_z[rows(y * 128 + z * R, R)] = p_ref[:, stripe(LINE + z)]
    arrived(META1, "y", lambda s: meta_y.at[s])
    push(META2, "z", lambda t: meta_y, lambda s: meta_all.at[s])

    def block(store, n):
        return store.at[rows(n % LINE * 128, 128)]

    def hand(phase, axis, store, n, t, follow):
        ref = block(store, n)
        op = pltpu.make_async_remote_copy(
            src_ref=ref, dst_ref=ref, send_sem=send_sem.at[follow, t % LINE], recv_sem=recv_sem.at[phase, n % LINE],
            device_id=target(axis, t % LINE), device_id_type=MESH,
        )
        op.start()
        started.append(op)

    def landed(phase, axis, store, n):
        copy(phase, axis, n % LINE, block(store, n), block(store, n), n % LINE).wait_recv()

    arrived(SPREAD_Y, "y", lambda s: store_y.at[rows(z * 128 + s * R, R)])
    for d in (2, 6, 1, 7):
        hand(FWD_Y, "z", store_y, z, z + d, FWD_Y)
    arrived(SPREAD_Z, "z", lambda s: store_z.at[rows(y * 128 + s * R, R)])
    for d in (2, 6, 1, 7):
        hand(FWD_Z, "y", store_z, y, y + d, FWD_Z)

    meta_all[z] = meta_y[...]
    arrived(META2, "z", lambda s: meta_all.at[s])
    for s in range(LINE):
        for t in range(LINE):
            table[pl.ds(t * LINE + s, 1), :] = meta_all[s, t]
    rows_of = table[:, :128].astype(F32)
    index_of = table[:, 128:].astype(F32)
    source = iota((64, 128), 0)
    lane = iota((64, 128), 1)
    remote = want - R
    total = jnp.zeros((64, 128), F32)
    for s in range(LINE):
        column = jnp.sum(jnp.where(lane == y % 2 * 64 + z * LINE + s, rows_of, 0.0), axis=1, keepdims=True)
        value = column + (source * R).astype(F32)
        total = total + jnp.where(source * LINE + s == remote, value, 0.0)
    fine = jnp.where(want < R, want + row * R, jnp.sum(total, axis=0, keepdims=True).astype(I32))
    request[...] = fine
    req_y[y] = fine
    req_z[z] = fine
    push(REQ_Y, "y", lambda t: request, lambda s: req_y.at[s])
    push(REQ_Z, "z", lambda t: request, lambda s: req_z.at[s])
    for d in (6, 2):
        for phase, follow, axis, store in ((FWD_Y, NEXT_Y, "z", store_y), (FWD_Z, NEXT_Z, "y", store_z)):
            me = place[axis]
            landed(phase, axis, store, me + d)
            if d == 6:
                hand(phase, axis, store, me + 6, me + 2, follow)
            hand(phase, axis, store, me + d, me + 8 - d // 2 if d == 2 else me + 1, follow)
    total = jnp.zeros((64, 128), F32)
    for t in range(R):
        total = total + jnp.where(source * R + t == fine, index_of[:, t : t + 1], 0.0)
    half_of = jnp.sum(total, axis=0, keepdims=True)

    def make_pick(n, _):
        r = iota((128, 1), 0)
        col = (r & 63)
        f = ((r >> 6) & 1) * 512 + (col & 1) * 256 + (col >> 2) * 16 + ((col >> 1) & 1) * 8 + n
        pick[rows(n * 128, 128), :] = jnp.where(iota((128, 1024), 1) == f, 1.0, 0.0).astype(BF16)
        return 0

    lax.fori_loop(0, 8, make_pick, 0)

    load.wait()
    for k in range(K):
        for w in range(32):
            tall[w * R : w * R + R, k * 128 : k * 128 + 128] = raw[k, :, w * 128 : w * 128 + 128]
    for k in range(K):
        at = slice(k * 128, k * 128 + 128)
        natural[:, at] = jnp.dot(order[...], tall[:, at], preferred_element_type=F32).astype(BF16)
    nothing = jnp.zeros((32, 128), BF16)
    for j in range(ASKED):
        b, slot = j // 8, j % 8
        i, k = j // FAR, 1 + j % FAR
        at = slice(slot * 128, slot * 128 + 128)
        here = b * 64 + (i - 8 * b // FAR) * 32
        there = 2 * b * 64 + 32 - here
        spread[here : here + 32, at] = natural[i * 32 : i * 32 + 32, k * 128 : k * 128 + 128]
        spread[there : there + 32, at] = nothing
    for n in range(4):
        terms[n] = jnp.dot(
            spread[...], pick[:, n * 256 : n * 256 + 256], preferred_element_type=F32
        ).astype(BF16)

    left = iota((128, 128), 1) < 64

    def join(out, count):
        both = []
        for pr in range(2):
            u0, u1 = (out[(2 * pr + n) * count : (2 * pr + n + 1) * count] for n in range(2))
            v0, v1 = (out[(4 + 2 * pr + n) * count : (5 + 2 * pr + n) * count] for n in range(2))
            both.append(jnp.where(left[:count], u0 + pltpu.roll(u1, 64, 1), pltpu.roll(v0, 64, 1) + v1))
        return both

    r = iota((512, 1), 0)
    f = ((r >> 6) & 1) * 256 + (r & 1) * 128 + (r >> 7) * 32 + ((r & 63) >> 1)
    own_pick[...] = jnp.where(iota((512, 512), 1) == f, 1.0, 0.0).astype(BF16)
    own_spread[...] = jnp.zeros_like(own_spread)
    for i in range(R):
        own_spread[i * 32 : i * 32 + 32, i % 4 * 128 : i % 4 * 128 + 128] = natural[i * 32 : i * 32 + 32, :128]
    own_terms[...] = jnp.dot(own_spread[...], own_pick[...], preferred_element_type=F32).astype(BF16)
    upper = idx_all[c]
    for q in range(4):
        at = slice(q * 128, q * 128 + 128)
        pieces = []
        for m in (1.0 - upper[:, at], upper[:, at]):
            for n in range(4):
                pieces.append(own_terms[at, n * 128 : n * 128 + 128] * m.astype(BF16))
        out = jnp.dot(jnp.concatenate(pieces, axis=0), own[at], preferred_element_type=F32)
        for pr, value in enumerate(join(out, 128)):
            ap[pr, at, :] = value

    eye = iota((128, 128), 0) == iota((128, 128), 1)

    def seek(req, hot, axis, swap):
        n = iota((1, 1024), 1)
        if swap:
            n = ((n >> 4) & 7) * 128 + (n >> 7) * R + (n & 15)

        def one(t, _):
            column = jnp.sum(jnp.where(eye, req[t], 0).astype(F32), axis=1, keepdims=True)[:ASKED].astype(I32)
            hot[t] = jnp.where(n == column, 1.0, 0.0).astype(BF16)
            return 0

        lax.fori_loop(0, LINE, one, 0)

    def serve(hot, t, store):
        got = jnp.dot(hot[t], store[...], preferred_element_type=F32).reshape(GROUPS, 8, 256)
        return jnp.concatenate([got[:, :, :128], got[:, :, 128:]], axis=1).astype(BF16)

    arrived(REQ_Y, "y", lambda s: req_y.at[s])
    arrived(REQ_Z, "z", lambda s: req_z.at[s])
    seek(req_y, hot_y, "y", True)
    seek(req_z, hot_z, "z", False)
    for d in (1, 7, 3, 5, 4):
        landed(FWD_Y, "z", store_y, z + d)
        landed(FWD_Z, "y", store_z, y + d)
    for d in (4, 3, 5, 2, 6, 1, 7):
        t = (y + d) % LINE
        pack_y[t] = serve(hot_y, t, store_y)
        op = copy(GHOST_Y, "y", t, pack_y.at[t], ghost.at[:, rows(y * 16, 16), :], y)
        op.start()
        started.append(op)
        t = (z + d) % LINE
        pack_z[t] = serve(hot_z, t, store_z)
        op = copy(GHOST_Z, "z", t, pack_z.at[t], ghost.at[:, rows(128 + z * 16, 16), :], z)
        op.start()
        started.append(op)
    ghost[:, rows(y * 16, 16), :] = serve(hot_y, y, store_y)
    ghost[:, rows(128 + z * 16, 16), :] = serve(hot_z, z, store_z)

    by_group = jnp.where(iota((16, 128), 1) >> 3 == iota((16, 128), 0), half_of, 0.0)
    by_slot = jnp.where((iota((128, 256), 0) & 7) == (iota((128, 256), 1) & 7), 1.0, 0.0)
    mask = jnp.dot(by_group.astype(BF16), by_slot.astype(BF16), preferred_element_type=F32)
    for b in range(GROUPS):
        upper = mask[b : b + 1]
        for h, m in ((0, 1.0 - upper), (1, upper)):
            for n in range(4):
                lhs[b, h * 256 + n * 64 : h * 256 + n * 64 + 64, :] = (
                    terms[n, b * 64 : b * 64 + 64, :] * m.astype(BF16)
                )
    arrived(PANEL, "c", lambda s: panel.at[s])
    arrived(PINDEX, "c", lambda s: idx_all.at[s])

    def make_wide(n, _):
        upper = idx_all[n]
        for h, m in ((0, 1.0 - upper), (1, upper)):
            for pr in range(2):
                wide[rows(n * 128 + h * 64, 64), pr * 512 : pr * 512 + 512] = (
                    panel[n, pr * 64 : pr * 64 + 64, :] * m.astype(BF16)
                )
        return 0

    lax.fori_loop(0, LINE, make_wide, 0)

    arrived(GHOST_Y, "y", lambda s: ghost.at[:, rows(s * 16, 16), :])
    arrived(GHOST_Z, "z", lambda s: ghost.at[:, rows(128 + s * 16, 16), :])

    for b in range(GROUPS):
        out = jnp.dot(lhs[b], ghost[b], preferred_element_type=F32)
        start = 8 * b // FAR * 32
        for pr, value in enumerate(join(out, 64)):
            ap[pr, start : start + 64, :] += value
    for pr in range(2):
        apb[pr * 512 : pr * 512 + 512] = ap[pr].astype(BF16)

    for n in range(LINE):
        value = jnp.dot(wide[n * 128 : n * 128 + 128, :], apb[...], preferred_element_type=F32)
        value = value.reshape(LINE, 2, 8, 128)
        partial[n] = value
        send_y[n] = value[:, 0].reshape(64, 128).astype(BF16)
    push(SUM_Y, "y", lambda t: send_y.at[t], lambda s: sum_y.at[s])
    for n in range(LINE):
        send_z[n] = partial[:, n, 1].reshape(64, 128).astype(BF16)
    push(SUM_Z, "z", lambda t: send_z.at[t], lambda s: sum_z.at[s])
    arrived(SUM_Y, "y", lambda s: sum_y.at[s])
    acc = partial[y, :, 0].reshape(64, 128)
    for t in others("y"):
        acc = acc + sum_y[t].astype(F32)
    half_y[...] = acc.reshape(LINE, 8, 128)
    push(LAST_Y, "z", lambda t: half_y.at[t], lambda s: last_y.at[s])
    arrived(SUM_Z, "z", lambda s: sum_z.at[s])
    acc = partial[:, z, 1].reshape(64, 128)
    for t in others("z"):
        acc = acc + sum_z[t].astype(F32)
    half_z[...] = acc.reshape(LINE, 8, 128)
    push(LAST_Z, "y", lambda t: half_z.at[t], lambda s: last_z.at[s])
    arrived(LAST_Y, "z", lambda s: last_y.at[s])
    acc = half_y[z]
    for t in others("z"):
        acc = acc + last_y[t]
    out_ref[0:8] = acc
    arrived(LAST_Z, "y", lambda s: last_z.at[s])
    acc = half_z[y]
    for t in others("y"):
        acc = acc + last_z[t]
    out_ref[8:16] = acc
    for op in started:
        op.wait_send()


def shards(a_tiles, neighbors, send_rows, p_tiles, p_index):
    vmem = pl.BlockSpec(memory_space=pltpu.VMEM)
    V = pltpu.VMEM
    return pl.pallas_call(
        kernel,
        out_shape=jax.ShapeDtypeStruct((R, 128), F32),
        in_specs=[vmem, pl.BlockSpec(memory_space=pl.ANY), vmem, vmem, vmem],
        out_specs=vmem,
        scratch_shapes=[
            V((K, R, 4096), BF16), V((LINE, 1, 256), I32),
            V((1024, 256), BF16), V((1024, 256), BF16),
            V((LINE, 1, 256), I32), V((LINE, LINE, 1, 256), I32), V((64, 256), I32),
            V((1, 128), I32), V((LINE, 1, 128), I32), V((LINE, 1, 128), I32),
            V((LINE, ASKED, 1024), BF16), V((LINE, ASKED, 1024), BF16),
            V((LINE, GROUPS, 16, 128), BF16), V((LINE, GROUPS, 16, 128), BF16),
            V((GROUPS, 256, 128), BF16),
            V((LINE, 128, 512), BF16), V((LINE, 1, 512), F32),
            V((512, 512), BF16), V((512, 1024), BF16), V((512, K * 128), BF16), V((512, 128), BF16),
            V((1024, 1024), BF16), V((GROUPS * 64, 1024), BF16), V((4, GROUPS * 64, 256), BF16),
            V((GROUPS, 512, 256), BF16), V((1024, 1024), BF16),
            V((512, 512), BF16), V((512, 512), BF16), V((512, 512), BF16),
            V((2, 512, 128), F32), V((1024, 128), BF16), V((LINE, LINE, 2, 8, 128), F32),
            V((LINE, 64, 128), BF16), V((LINE, 64, 128), BF16),
            V((LINE, 64, 128), BF16), V((LINE, 64, 128), BF16),
            V((LINE, 8, 128), F32), V((LINE, 8, 128), F32),
            V((LINE, 8, 128), F32), V((LINE, 8, 128), F32),
            pltpu.SemaphoreType.DMA((18, LINE)), pltpu.SemaphoreType.DMA((16, LINE)), pltpu.SemaphoreType.DMA,
        ],
        compiler_params=pltpu.CompilerParams(
            collective_id=0, has_side_effects=True, vmem_limit_bytes=48 * 2**20
        ),
    )(
        p_tiles.reshape(R, 4096),
        a_tiles.transpose(1, 0, 2),
        neighbors.T,
        send_rows,
        p_index.reshape(1, R),
    )


def solution(mesh):
    in_specs = (
        P("row", None, None),
        P("row", None),
        P("row", None),
        P("row", "col", None),
        P("row", "col"),
    )
    return jax.shard_map(shards, mesh=mesh, in_specs=in_specs, out_specs=P("row", "col"), check_vma=False)
```

```python
import functools

import jax
import jax.numpy as jnp
from jax import lax
from jax.experimental import pallas as pl
from jax.experimental.pallas import tpu as pltpu
from jax.sharding import PartitionSpec as P

MESH = pl.DeviceIdType.MESH
LINE = 8
R = 16
K = 7
FAR = K - 1
ASKED = R * FAR
GROUPS = ASKED // 8
F32, BF16, I32 = jnp.float32, jnp.bfloat16, jnp.int32
META1, SPREAD_Y, SPREAD_Z, PANEL, PINDEX, META2, REQ_Y, REQ_Z, GHOST_Y, GHOST_Z, SUM_Y, SUM_Z, LAST_Y, LAST_Z = range(14)


def iota(shape, dim):
    return lax.broadcasted_iota(I32, shape, dim)


def kernel(
    p_ref, a_ref, near_in, sends_in, index_in, out_ref,
    near_ref, sends_ref, index_ref,
    raw, mine, meta, store_y, store_z, meta_y, meta_all, table, request, req_y, req_z, hot_y, hot_z,
    pack_y, pack_z, ghost, panel, idx_all, order, tall, natural, own, pick, spread, terms, lhs, wide,
    own_pick, own_spread, own_terms,
    ap, apb, partial, send_y, send_z, sum_y, sum_z, half_y, half_z, last_y, last_z,
    send_sem, recv_sem, leg_sem, part_sem, next_sem, far_sem, block_sem, local_sem,
):
    row, c = lax.axis_index("row"), lax.axis_index("col")
    y, z = row // LINE, row % LINE
    place = {"y": y, "z": z, "c": c}

    def target(axis, t):
        if axis == "y":
            return (t * LINE + z, c)
        if axis == "z":
            return (y * LINE + t, c)
        return (row, t)

    def others(axis):
        return [(place[axis] + d) % LINE for d in range(1, LINE)]

    def copy(phase, axis, t, src, dst, mine):
        return pltpu.make_async_remote_copy(
            src_ref=src, dst_ref=dst, send_sem=send_sem.at[phase, t], recv_sem=recv_sem.at[phase, mine],
            device_id=target(axis, t), device_id_type=MESH,
        )

    started = []

    def push(phase, axis, src, dst):
        me = place[axis]
        for t in others(axis):
            op = copy(phase, axis, t, src(t), dst(me), me)
            op.start()
            started.append(op)

    def arrived(phase, axis, dst):
        for t in others(axis):
            copy(phase, axis, t, dst(t), dst(t), t).wait_recv()

    barrier = pltpu.get_barrier_semaphore()
    for axis in ("y", "z", "c"):
        for t in others(axis):
            pl.semaphore_signal(barrier, inc=1, device_id=target(axis, t), device_id_type=MESH)
    load = pltpu.make_async_copy(a_ref, raw, local_sem.at[0])
    fetch = pltpu.make_async_copy(p_ref, mine, local_sem.at[1])
    small = [
        pltpu.make_async_copy(src, dst, local_sem.at[2 + n])
        for n, (src, dst) in enumerate(((sends_in, sends_ref), (index_in, index_ref), (near_in, near_ref)))
    ]
    for op in small + [fetch, load]:
        op.start()
    small[0].wait()
    small[1].wait()

    for t in range(LINE):
        meta[t, :, :128] = sends_ref[:, t // 2 * 128 : t // 2 * 128 + 128]
        meta[t, :, 128:] = jnp.zeros((1, 128), I32)
        meta[t, :, 128 : 128 + R] = index_ref[...]
    pl.semaphore_wait(barrier, 3 * (LINE - 1))

    def stripe(s):
        return pl.ds(pl.multiple_of(s * 256, 256), 256)

    def rows(start, count):
        return pl.ds(pl.multiple_of(start, count), count)

    push(META1, "y", lambda t: meta.at[t], lambda s: meta_y.at[s])
    push(SPREAD_Y, "y", lambda t: p_ref.at[:, stripe(t)], lambda s: store_y.at[rows(z * 128 + s * R, R)])
    push(SPREAD_Z, "z", lambda t: p_ref.at[:, stripe(LINE + t)], lambda s: store_z.at[rows(y * 128 + s * R, R)])
    meta_y[y] = meta[y]
    fetch.wait()
    store_y[rows(z * 128 + y * R, R)] = mine[:, stripe(y)]
    store_z[rows(y * 128 + z * R, R)] = mine[:, stripe(LINE + z)]
    arrived(META1, "y", lambda s: meta_y.at[s])
    push(META2, "z", lambda t: meta_y, lambda s: meta_all.at[s])

    roles = ((store_y, "z", z), (store_z, "y", y))

    def part(role, n, h):
        return roles[role][0].at[rows(n % LINE * 128 + h * 64, 64)]

    def block(role, n):
        return roles[role][0].at[rows(n % LINE * 128, 128)]

    def hand(role, ref, leg, step, recv):
        _, axis, me = roles[role]
        op = pltpu.make_async_remote_copy(
            src_ref=ref, dst_ref=ref, send_sem=leg_sem.at[role, leg], recv_sem=recv,
            device_id=target(axis, (me + step) % LINE), device_id_type=MESH,
        )
        op.start()
        started.append(op)

    def await_ref(role, ref, recv):
        _, axis, me = roles[role]
        pltpu.make_async_remote_copy(
            src_ref=ref, dst_ref=ref, send_sem=leg_sem.at[role, 0], recv_sem=recv,
            device_id=target(axis, (me + 1) % LINE), device_id_type=MESH,
        ).wait_recv()

    def first(role):
        me = roles[role][2]
        hand(role, part(role, me, 0), 0, 2, part_sem.at[role, 0, 0])
        hand(role, part(role, me, 1), 1, 6, part_sem.at[role, 1, 1])
        hand(role, part(role, me, 1), 2, 2, part_sem.at[role, 0, 1])
        hand(role, part(role, me, 0), 3, 6, part_sem.at[role, 1, 0])
        hand(role, block(role, me), 4, 1, block_sem.at[role, me])
        hand(role, block(role, me), 5, 7, block_sem.at[role, me])

    def second(role, back, h):
        me = roles[role][2]
        n, onward, far = (me + 6, 1, 2) if back == 0 else (me + 2, 7, 6)
        ref = part(role, n, h)
        await_ref(role, ref, part_sem.at[role, back, h])
        if h == back:
            hand(role, ref, 6 + back, far, far_sem.at[role, h])
        hand(role, ref, 8 + 2 * back + h, onward, next_sem.at[role, back, h])

    def landed(role):
        me = roles[role][2]
        for d in (1, 7):
            await_ref(role, block(role, me + d), block_sem.at[role, (me + d) % LINE])
        for h in range(2):
            await_ref(role, part(role, me + 5, h), next_sem.at[role, 0, h])
            await_ref(role, part(role, me + 3, h), next_sem.at[role, 1, h])
            await_ref(role, part(role, me + 4, h), far_sem.at[role, h])

    arrived(SPREAD_Y, "y", lambda s: store_y.at[rows(z * 128 + s * R, R)])
    first(0)
    arrived(SPREAD_Z, "z", lambda s: store_z.at[rows(y * 128 + s * R, R)])
    first(1)

    indices = index_ref[...].astype(F32)
    small[2].wait()
    couple = near_ref[...]
    to_lane = jnp.where(
        (iota((R, FAR * 128), 1) & 127) == iota((R, FAR * 128), 0) * FAR + (iota((R, FAR * 128), 1) >> 7), 1.0, 0.0
    ).astype(BF16)
    high = jnp.dot((couple >> 4).astype(F32).astype(BF16), to_lane, preferred_element_type=F32)
    low = jnp.dot((couple & 15).astype(F32).astype(BF16), to_lane, preferred_element_type=F32)
    want = jnp.zeros((1, 128), F32)
    for k in range(FAR):
        at = slice(k * 128, k * 128 + 128)
        want = want + high[k + 1 : k + 2, at] * 16.0 + low[k + 1 : k + 2, at]
    want = want.astype(I32)
    widen = jnp.where(iota((R, 512), 1) >> 5 == iota((R, 512), 0), 1.0, 0.0).astype(BF16)
    idx_all[c] = jnp.dot(
        jnp.broadcast_to(indices, (8, R)).astype(BF16), widen, preferred_element_type=F32
    )[:1]
    r = iota((512, 1), 0)
    order[...] = jnp.where(iota((512, 512), 1) == (r & 31) * R + (r >> 5), 1.0, 0.0).astype(BF16)
    for w in range(32):
        tall[w * R : w * R + R, K * 128 :] = mine[:, w * 128 : w * 128 + 128]
    own[...] = jnp.dot(order[...], tall[:, K * 128 :], preferred_element_type=F32).astype(BF16)
    panel[c] = own[...].astype(F32).T.astype(BF16)
    push(PINDEX, "c", lambda t: idx_all.at[c], lambda s: idx_all.at[s])
    push(PANEL, "c", lambda t: panel.at[c], lambda s: panel.at[s])

    def make_pick(n, _):
        r = iota((128, 1), 0)
        col = (r & 63)
        f = ((r >> 6) & 1) * 512 + (col & 1) * 256 + (col >> 2) * 16 + ((col >> 1) & 1) * 8 + n
        pick[rows(n * 128, 128), :] = jnp.where(iota((128, 1024), 1) == f, 1.0, 0.0).astype(BF16)
        return 0

    lax.fori_loop(0, 8, make_pick, 0)

    r = iota((512, 1), 0)
    f = ((r >> 6) & 1) * 256 + (r & 1) * 128 + (r >> 7) * 32 + ((r & 63) >> 1)
    own_pick[...] = jnp.where(iota((512, 512), 1) == f, 1.0, 0.0).astype(BF16)

    meta_all[z] = meta_y[...]
    arrived(META2, "z", lambda s: meta_all.at[s])
    for s in range(LINE):
        for t in range(LINE):
            table[pl.ds(t * LINE + s, 1), :] = meta_all[s, t]
    rows_of = table[:, :128].astype(F32)
    index_of = table[:, 128:].astype(F32)
    source = iota((64, 128), 0)
    lane = iota((64, 128), 1)
    remote = want - R
    total = jnp.zeros((64, 128), F32)
    for s in range(LINE):
        column = jnp.sum(jnp.where(lane == y % 2 * 64 + z * LINE + s, rows_of, 0.0), axis=1, keepdims=True)
        value = column + (source * R).astype(F32)
        total = total + jnp.where(source * LINE + s == remote, value, 0.0)
    fine = jnp.where(want < R, want + row * R, jnp.sum(total, axis=0, keepdims=True).astype(I32))
    request[...] = fine
    req_y[y] = fine
    req_z[z] = fine
    push(REQ_Y, "y", lambda t: request, lambda s: req_y.at[s])
    push(REQ_Z, "z", lambda t: request, lambda s: req_z.at[s])
    for back, h in ((0, 0), (1, 1), (0, 1), (1, 0)):
        for role in range(2):
            second(role, back, h)
    total = jnp.zeros((64, 128), F32)
    for t in range(R):
        total = total + jnp.where(source * R + t == fine, index_of[:, t : t + 1], 0.0)
    half_of = jnp.sum(total, axis=0, keepdims=True)

    load.wait()
    for k in range(K):
        for w in range(32):
            tall[w * R : w * R + R, k * 128 : k * 128 + 128] = raw[k, :, w * 128 : w * 128 + 128]
    for k in range(K):
        at = slice(k * 128, k * 128 + 128)
        natural[:, at] = jnp.dot(order[...], tall[:, at], preferred_element_type=F32).astype(BF16)
    nothing = jnp.zeros((32, 128), BF16)
    for j in range(ASKED):
        b, slot = j // 8, j % 8
        i, k = j // FAR, 1 + j % FAR
        at = slice(slot * 128, slot * 128 + 128)
        here = b * 64 + (i - 8 * b // FAR) * 32
        there = 2 * b * 64 + 32 - here
        spread[here : here + 32, at] = natural[i * 32 : i * 32 + 32, k * 128 : k * 128 + 128]
        spread[there : there + 32, at] = nothing
    for n in range(4):
        terms[n] = jnp.dot(
            spread[...], pick[:, n * 256 : n * 256 + 256], preferred_element_type=F32
        ).astype(BF16)

    left = iota((128, 128), 1) < 64

    def join(out, count):
        both = []
        for pr in range(2):
            u0, u1 = (out[(2 * pr + n) * count : (2 * pr + n + 1) * count] for n in range(2))
            v0, v1 = (out[(4 + 2 * pr + n) * count : (5 + 2 * pr + n) * count] for n in range(2))
            both.append(jnp.where(left[:count], u0 + pltpu.roll(u1, 64, 1), pltpu.roll(v0, 64, 1) + v1))
        return both

    own_spread[...] = jnp.zeros_like(own_spread)
    for i in range(R):
        own_spread[i * 32 : i * 32 + 32, i % 4 * 128 : i % 4 * 128 + 128] = natural[i * 32 : i * 32 + 32, :128]
    own_terms[...] = jnp.dot(own_spread[...], own_pick[...], preferred_element_type=F32).astype(BF16)
    upper = idx_all[c]
    for q in range(4):
        at = slice(q * 128, q * 128 + 128)
        pieces = []
        for m in (1.0 - upper[:, at], upper[:, at]):
            for n in range(4):
                pieces.append(own_terms[at, n * 128 : n * 128 + 128] * m.astype(BF16))
        out = jnp.dot(jnp.concatenate(pieces, axis=0), own[at], preferred_element_type=F32)
        for pr, value in enumerate(join(out, 128)):
            ap[pr, at, :] = value

    eye = iota((128, 128), 0) == iota((128, 128), 1)

    def seek(req, hot, axis, swap):
        n = iota((1, 1024), 1)
        if swap:
            n = ((n >> 4) & 7) * 128 + (n >> 7) * R + (n & 15)

        def one(t, _):
            column = jnp.sum(jnp.where(eye, req[t], 0).astype(F32), axis=1, keepdims=True)[:ASKED].astype(I32)
            hot[t] = jnp.where(n == column, 1.0, 0.0).astype(BF16)
            return 0

        lax.fori_loop(0, LINE, one, 0)

    def serve(hot, t, store):
        got = jnp.dot(hot[t], store[...], preferred_element_type=F32).reshape(GROUPS, 8, 256)
        return jnp.concatenate([got[:, :, :128], got[:, :, 128:]], axis=1).astype(BF16)

    arrived(REQ_Y, "y", lambda s: req_y.at[s])
    arrived(REQ_Z, "z", lambda s: req_z.at[s])
    seek(req_y, hot_y, "y", True)
    seek(req_z, hot_z, "z", False)
    for role in range(2):
        landed(role)
    for d in (4, 3, 5, 2, 6, 1, 7):
        t = (y + d) % LINE
        pack_y[t] = serve(hot_y, t, store_y)
        op = copy(GHOST_Y, "y", t, pack_y.at[t], ghost.at[:, rows(y * 16, 16), :], y)
        op.start()
        started.append(op)
        t = (z + d) % LINE
        pack_z[t] = serve(hot_z, t, store_z)
        op = copy(GHOST_Z, "z", t, pack_z.at[t], ghost.at[:, rows(128 + z * 16, 16), :], z)
        op.start()
        started.append(op)
    ghost[:, rows(y * 16, 16), :] = serve(hot_y, y, store_y)
    ghost[:, rows(128 + z * 16, 16), :] = serve(hot_z, z, store_z)

    by_group = jnp.where(iota((16, 128), 1) >> 3 == iota((16, 128), 0), half_of, 0.0)
    by_slot = jnp.where((iota((128, 256), 0) & 7) == (iota((128, 256), 1) & 7), 1.0, 0.0)
    mask = jnp.dot(by_group.astype(BF16), by_slot.astype(BF16), preferred_element_type=F32)
    for b in range(GROUPS):
        upper = mask[b : b + 1]
        for h, m in ((0, 1.0 - upper), (1, upper)):
            for n in range(4):
                lhs[b, h * 256 + n * 64 : h * 256 + n * 64 + 64, :] = (
                    terms[n, b * 64 : b * 64 + 64, :] * m.astype(BF16)
                )
    arrived(PANEL, "c", lambda s: panel.at[s])
    arrived(PINDEX, "c", lambda s: idx_all.at[s])

    def make_wide(n, _):
        upper = idx_all[n]
        for h, m in ((0, 1.0 - upper), (1, upper)):
            for pr in range(2):
                wide[rows(n * 128 + h * 64, 64), pr * 512 : pr * 512 + 512] = (
                    panel[n, pr * 64 : pr * 64 + 64, :] * m.astype(BF16)
                )
        return 0

    lax.fori_loop(0, LINE, make_wide, 0)

    arrived(GHOST_Y, "y", lambda s: ghost.at[:, rows(s * 16, 16), :])
    arrived(GHOST_Z, "z", lambda s: ghost.at[:, rows(128 + s * 16, 16), :])

    for b in range(GROUPS):
        out = jnp.dot(lhs[b], ghost[b], preferred_element_type=F32)
        start = 8 * b // FAR * 32
        for pr, value in enumerate(join(out, 64)):
            ap[pr, start : start + 64, :] += value
    for pr in range(2):
        apb[pr * 512 : pr * 512 + 512] = ap[pr].astype(BF16)

    for n in range(LINE):
        value = jnp.dot(wide[n * 128 : n * 128 + 128, :], apb[...], preferred_element_type=F32)
        value = value.reshape(LINE, 2, 8, 128)
        partial[n] = value
        send_y[n] = value[:, 0].reshape(64, 128).astype(BF16)
    push(SUM_Y, "y", lambda t: send_y.at[t], lambda s: sum_y.at[s])
    for n in range(LINE):
        send_z[n] = partial[:, n, 1].reshape(64, 128).astype(BF16)
    push(SUM_Z, "z", lambda t: send_z.at[t], lambda s: sum_z.at[s])
    arrived(SUM_Y, "y", lambda s: sum_y.at[s])
    acc = partial[y, :, 0].reshape(64, 128)
    for t in others("y"):
        acc = acc + sum_y[t].astype(F32)
    half_y[...] = acc.reshape(LINE, 8, 128)
    push(LAST_Y, "z", lambda t: half_y.at[t], lambda s: last_y.at[s])
    arrived(SUM_Z, "z", lambda s: sum_z.at[s])
    acc = partial[:, z, 1].reshape(64, 128)
    for t in others("z"):
        acc = acc + sum_z[t].astype(F32)
    half_z[...] = acc.reshape(LINE, 8, 128)
    push(LAST_Z, "y", lambda t: half_z.at[t], lambda s: last_z.at[s])
    arrived(LAST_Y, "z", lambda s: last_y.at[s])
    acc = half_y[z]
    for t in others("z"):
        acc = acc + last_y[t]
    out_ref[0:8] = acc
    arrived(LAST_Z, "y", lambda s: last_z.at[s])
    acc = half_z[y]
    for t in others("y"):
        acc = acc + last_z[t]
    out_ref[8:16] = acc
    for op in started:
        op.wait_send()


def shards(a_tiles, neighbors, send_rows, p_tiles, p_index):
    vmem = pl.BlockSpec(memory_space=pltpu.VMEM)
    V = pltpu.VMEM
    return pl.pallas_call(
        kernel,
        out_shape=jax.ShapeDtypeStruct((R, 128), F32),
        in_specs=[pl.BlockSpec(memory_space=pl.ANY)] * 5,
        out_specs=vmem,
        scratch_shapes=[
            V((K, R), I32), V((1, LINE * 64), I32), V((1, R), I32),
            V((K, R, 4096), BF16), V((R, 4096), BF16), V((LINE, 1, 256), I32),
            V((1024, 256), BF16), V((1024, 256), BF16),
            V((LINE, 1, 256), I32), V((LINE, LINE, 1, 256), I32), V((64, 256), I32),
            V((1, 128), I32), V((LINE, 1, 128), I32), V((LINE, 1, 128), I32),
            V((LINE, ASKED, 1024), BF16), V((LINE, ASKED, 1024), BF16),
            V((LINE, GROUPS, 16, 128), BF16), V((LINE, GROUPS, 16, 128), BF16),
            V((GROUPS, 256, 128), BF16),
            V((LINE, 128, 512), BF16), V((LINE, 1, 512), F32),
            V((512, 512), BF16), V((512, 1024), BF16), V((512, K * 128), BF16), V((512, 128), BF16),
            V((1024, 1024), BF16), V((GROUPS * 64, 1024), BF16), V((4, GROUPS * 64, 256), BF16),
            V((GROUPS, 512, 256), BF16), V((1024, 1024), BF16),
            V((512, 512), BF16), V((512, 512), BF16), V((512, 512), BF16),
            V((2, 512, 128), F32), V((1024, 128), BF16), V((LINE, LINE, 2, 8, 128), F32),
            V((LINE, 64, 128), BF16), V((LINE, 64, 128), BF16),
            V((LINE, 64, 128), BF16), V((LINE, 64, 128), BF16),
            V((LINE, 8, 128), F32), V((LINE, 8, 128), F32),
            V((LINE, 8, 128), F32), V((LINE, 8, 128), F32),
            pltpu.SemaphoreType.DMA((14, LINE)), pltpu.SemaphoreType.DMA((14, LINE)),
            pltpu.SemaphoreType.DMA((2, 12)), pltpu.SemaphoreType.DMA((2, 2, 2)), pltpu.SemaphoreType.DMA((2, 2, 2)),
            pltpu.SemaphoreType.DMA((2, 2)), pltpu.SemaphoreType.DMA((2, LINE)), pltpu.SemaphoreType.DMA((5,)),
        ],
        compiler_params=pltpu.CompilerParams(
            collective_id=0, has_side_effects=True, vmem_limit_bytes=56 * 2**20
        ),
    )(
        p_tiles.reshape(R, 4096),
        a_tiles.transpose(1, 0, 2),
        neighbors.T,
        send_rows,
        p_index.reshape(1, R),
    )


def solution(mesh):
    in_specs = (
        P("row", None, None),
        P("row", None),
        P("row", None),
        P("row", "col", None),
        P("row", "col"),
    )
    return jax.shard_map(shards, mesh=mesh, in_specs=in_specs, out_specs=P("row", "col"), check_vma=False)
```

```python
import functools

import jax
import jax.numpy as jnp
from jax import lax
from jax.experimental import pallas as pl
from jax.experimental.pallas import tpu as pltpu
from jax.sharding import PartitionSpec as P

MESH = pl.DeviceIdType.MESH
LINE = 8
R = 16
K = 7
FAR = K - 1
ASKED = R * FAR
GROUPS = ASKED // 8
F32, BF16, I32 = jnp.float32, jnp.bfloat16, jnp.int32
META1, SPREAD_Y, SPREAD_Z, PANEL, PINDEX, META2, REQ_Y, REQ_Z, GHOST_Y, GHOST_Z, SUM_Y, SUM_Z, LAST_Y, LAST_Z = range(14)


def iota(shape, dim):
    return lax.broadcasted_iota(I32, shape, dim)


def kernel(
    p_ref, a_ref, near_in, sends_in, index_in, out_ref,
    near_ref, sends_ref, index_ref,
    raw, mine, meta, store_y, store_z, meta_y, meta_all, table, request, req_y, req_z, hot_y, hot_z,
    pack_y, pack_z, ghost, panel, idx_all, order, tall, natural, own, pick, spread, terms, lhs, wide,
    own_pick, own_spread, own_terms,
    ap, apb, partial, send_y, send_z, sum_y, sum_z, half_y, half_z, last_y, last_z,
    send_sem, recv_sem, leg_sem, part_sem, next_sem, far_sem, block_sem, local_sem,
):
    row, c = lax.axis_index("row"), lax.axis_index("col")
    y, z = row // LINE, row % LINE
    place = {"y": y, "z": z, "c": c}

    def target(axis, t):
        if axis == "y":
            return (t * LINE + z, c)
        if axis == "z":
            return (y * LINE + t, c)
        return (row, t)

    def others(axis):
        return [(place[axis] + d) % LINE for d in range(1, LINE)]

    def copy(phase, axis, t, src, dst, mine):
        return pltpu.make_async_remote_copy(
            src_ref=src, dst_ref=dst, send_sem=send_sem.at[phase, t], recv_sem=recv_sem.at[phase, mine],
            device_id=target(axis, t), device_id_type=MESH,
        )

    started = []

    def push(phase, axis, src, dst):
        me = place[axis]
        for t in others(axis):
            op = copy(phase, axis, t, src(t), dst(me), me)
            op.start()
            started.append(op)

    def arrived(phase, axis, dst):
        for t in others(axis):
            copy(phase, axis, t, dst(t), dst(t), t).wait_recv()

    barrier = pltpu.get_barrier_semaphore()
    for axis in ("y", "z", "c"):
        for t in others(axis):
            pl.semaphore_signal(barrier, inc=1, device_id=target(axis, t), device_id_type=MESH)
    load = pltpu.make_async_copy(a_ref, raw, local_sem.at[0])
    fetch = pltpu.make_async_copy(p_ref, mine, local_sem.at[1])
    small = [
        pltpu.make_async_copy(src, dst, local_sem.at[2 + n])
        for n, (src, dst) in enumerate(((sends_in, sends_ref), (index_in, index_ref), (near_in, near_ref)))
    ]
    for op in small + [fetch, load]:
        op.start()
    small[0].wait()
    small[1].wait()

    for t in range(LINE):
        meta[t, :, :128] = sends_ref[:, t // 2 * 128 : t // 2 * 128 + 128]
        meta[t, :, 128:] = jnp.zeros((1, 128), I32)
        meta[t, :, 128 : 128 + R] = index_ref[...]
    pl.semaphore_wait(barrier, 3 * (LINE - 1))

    def stripe(s):
        return pl.ds(pl.multiple_of(s * 256, 256), 256)

    def rows(start, count):
        return pl.ds(pl.multiple_of(start, count), count)

    push(SPREAD_Y, "y", lambda t: p_ref.at[:, stripe(t)], lambda s: store_y.at[rows(z * 128 + s * R, R)])
    push(SPREAD_Z, "z", lambda t: p_ref.at[:, stripe(LINE + t)], lambda s: store_z.at[rows(y * 128 + s * R, R)])
    push(META1, "y", lambda t: meta.at[t], lambda s: meta_y.at[s])
    meta_y[y] = meta[y]
    fetch.wait()
    store_y[rows(z * 128 + y * R, R)] = mine[:, stripe(y)]
    store_z[rows(y * 128 + z * R, R)] = mine[:, stripe(LINE + z)]
    arrived(META1, "y", lambda s: meta_y.at[s])
    push(META2, "z", lambda t: meta_y, lambda s: meta_all.at[s])

    roles = ((store_y, "z", z), (store_z, "y", y))

    def part(role, n, h):
        return roles[role][0].at[rows(n % LINE * 128 + h * 64, 64)]

    def block(role, n):
        return roles[role][0].at[rows(n % LINE * 128, 128)]

    def hand(role, ref, leg, step, recv):
        _, axis, me = roles[role]
        op = pltpu.make_async_remote_copy(
            src_ref=ref, dst_ref=ref, send_sem=leg_sem.at[role, leg], recv_sem=recv,
            device_id=target(axis, (me + step) % LINE), device_id_type=MESH,
        )
        op.start()
        started.append(op)

    def await_ref(role, ref, recv):
        _, axis, me = roles[role]
        pltpu.make_async_remote_copy(
            src_ref=ref, dst_ref=ref, send_sem=leg_sem.at[role, 0], recv_sem=recv,
            device_id=target(axis, (me + 1) % LINE), device_id_type=MESH,
        ).wait_recv()

    def first(role):
        me = roles[role][2]
        hand(role, part(role, me, 0), 0, 2, part_sem.at[role, 0, 0])
        hand(role, part(role, me, 1), 1, 6, part_sem.at[role, 1, 1])
        hand(role, part(role, me, 1), 2, 2, part_sem.at[role, 0, 1])
        hand(role, part(role, me, 0), 3, 6, part_sem.at[role, 1, 0])
        hand(role, block(role, me), 4, 1, block_sem.at[role, me])
        hand(role, block(role, me), 5, 7, block_sem.at[role, me])

    def second(role, back, h):
        me = roles[role][2]
        n, onward, far = (me + 6, 1, 2) if back == 0 else (me + 2, 7, 6)
        ref = part(role, n, h)
        await_ref(role, ref, part_sem.at[role, back, h])
        if h == back:
            hand(role, ref, 6 + back, far, far_sem.at[role, h])
        hand(role, ref, 8 + 2 * back + h, onward, next_sem.at[role, back, h])

    def landed(role):
        me = roles[role][2]
        for d in (1, 7):
            await_ref(role, block(role, me + d), block_sem.at[role, (me + d) % LINE])
        for h in range(2):
            await_ref(role, part(role, me + 5, h), next_sem.at[role, 0, h])
            await_ref(role, part(role, me + 3, h), next_sem.at[role, 1, h])
            await_ref(role, part(role, me + 4, h), far_sem.at[role, h])

    arrived(SPREAD_Y, "y", lambda s: store_y.at[rows(z * 128 + s * R, R)])
    first(0)
    arrived(SPREAD_Z, "z", lambda s: store_z.at[rows(y * 128 + s * R, R)])
    first(1)

    indices = index_ref[...].astype(F32)
    small[2].wait()
    couple = near_ref[...]
    to_lane = jnp.where(
        (iota((R, FAR * 128), 1) & 127) == iota((R, FAR * 128), 0) * FAR + (iota((R, FAR * 128), 1) >> 7), 1.0, 0.0
    ).astype(BF16)
    high = jnp.dot((couple >> 4).astype(F32).astype(BF16), to_lane, preferred_element_type=F32)
    low = jnp.dot((couple & 15).astype(F32).astype(BF16), to_lane, preferred_element_type=F32)
    want = jnp.zeros((1, 128), F32)
    for k in range(FAR):
        at = slice(k * 128, k * 128 + 128)
        want = want + high[k + 1 : k + 2, at] * 16.0 + low[k + 1 : k + 2, at]
    want = want.astype(I32)
    widen = jnp.where(iota((R, 512), 1) >> 5 == iota((R, 512), 0), 1.0, 0.0).astype(BF16)
    idx_all[c] = jnp.dot(
        jnp.broadcast_to(indices, (8, R)).astype(BF16), widen, preferred_element_type=F32
    )[:1]
    r = iota((512, 1), 0)
    order[...] = jnp.where(iota((512, 512), 1) == (r & 31) * R + (r >> 5), 1.0, 0.0).astype(BF16)
    for w in range(32):
        tall[w * R : w * R + R, K * 128 :] = mine[:, w * 128 : w * 128 + 128]
    own[...] = jnp.dot(order[...], tall[:, K * 128 :], preferred_element_type=F32).astype(BF16)
    panel[c] = own[...].astype(F32).T.astype(BF16)
    push(PINDEX, "c", lambda t: idx_all.at[c], lambda s: idx_all.at[s])
    push(PANEL, "c", lambda t: panel.at[c], lambda s: panel.at[s])

    def make_pick(n, _):
        r = iota((128, 1), 0)
        col = (r & 63)
        f = ((r >> 6) & 1) * 512 + (col & 1) * 256 + (col >> 2) * 16 + ((col >> 1) & 1) * 8 + n
        pick[rows(n * 128, 128), :] = jnp.where(iota((128, 1024), 1) == f, 1.0, 0.0).astype(BF16)
        return 0

    lax.fori_loop(0, 8, make_pick, 0)

    r = iota((512, 1), 0)
    f = ((r >> 6) & 1) * 256 + (r & 1) * 128 + (r >> 7) * 32 + ((r & 63) >> 1)
    own_pick[...] = jnp.where(iota((512, 512), 1) == f, 1.0, 0.0).astype(BF16)

    meta_all[z] = meta_y[...]
    arrived(META2, "z", lambda s: meta_all.at[s])
    for s in range(LINE):
        for t in range(LINE):
            table[pl.ds(t * LINE + s, 1), :] = meta_all[s, t]
    rows_of = table[:, :128].astype(F32)
    index_of = table[:, 128:].astype(F32)
    source = iota((64, 128), 0)
    lane = iota((64, 128), 1)
    remote = want - R
    total = jnp.zeros((64, 128), F32)
    for s in range(LINE):
        column = jnp.sum(jnp.where(lane == y % 2 * 64 + z * LINE + s, rows_of, 0.0), axis=1, keepdims=True)
        value = column + (source * R).astype(F32)
        total = total + jnp.where(source * LINE + s == remote, value, 0.0)
    fine = jnp.where(want < R, want + row * R, jnp.sum(total, axis=0, keepdims=True).astype(I32))
    request[...] = fine
    req_y[y] = fine
    req_z[z] = fine
    push(REQ_Y, "y", lambda t: request, lambda s: req_y.at[s])
    push(REQ_Z, "z", lambda t: request, lambda s: req_z.at[s])
    for back, h in ((0, 0), (1, 1), (0, 1), (1, 0)):
        for role in range(2):
            second(role, back, h)
    total = jnp.zeros((64, 128), F32)
    for t in range(R):
        total = total + jnp.where(source * R + t == fine, index_of[:, t : t + 1], 0.0)
    half_of = jnp.sum(total, axis=0, keepdims=True)

    load.wait()
    for k in range(K):
        for w in range(32):
            tall[w * R : w * R + R, k * 128 : k * 128 + 128] = raw[k, :, w * 128 : w * 128 + 128]
    for k in range(K):
        at = slice(k * 128, k * 128 + 128)
        natural[:, at] = jnp.dot(order[...], tall[:, at], preferred_element_type=F32).astype(BF16)
    nothing = jnp.zeros((32, 128), BF16)
    for j in range(ASKED):
        b, slot = j // 8, j % 8
        i, k = j // FAR, 1 + j % FAR
        at = slice(slot * 128, slot * 128 + 128)
        here = b * 64 + (i - 8 * b // FAR) * 32
        there = 2 * b * 64 + 32 - here
        spread[here : here + 32, at] = natural[i * 32 : i * 32 + 32, k * 128 : k * 128 + 128]
        spread[there : there + 32, at] = nothing
    for n in range(4):
        terms[n] = jnp.dot(
            spread[...], pick[:, n * 256 : n * 256 + 256], preferred_element_type=F32
        ).astype(BF16)

    left = iota((128, 128), 1) < 64

    def join(out, count):
        both = []
        for pr in range(2):
            u0, u1 = (out[(2 * pr + n) * count : (2 * pr + n + 1) * count] for n in range(2))
            v0, v1 = (out[(4 + 2 * pr + n) * count : (5 + 2 * pr + n) * count] for n in range(2))
            both.append(jnp.where(left[:count], u0 + pltpu.roll(u1, 64, 1), pltpu.roll(v0, 64, 1) + v1))
        return both

    own_spread[...] = jnp.zeros_like(own_spread)
    for i in range(R):
        own_spread[i * 32 : i * 32 + 32, i % 4 * 128 : i % 4 * 128 + 128] = natural[i * 32 : i * 32 + 32, :128]
    own_terms[...] = jnp.dot(own_spread[...], own_pick[...], preferred_element_type=F32).astype(BF16)
    upper = idx_all[c]
    for q in range(4):
        at = slice(q * 128, q * 128 + 128)
        pieces = []
        for m in (1.0 - upper[:, at], upper[:, at]):
            for n in range(4):
                pieces.append(own_terms[at, n * 128 : n * 128 + 128] * m.astype(BF16))
        out = jnp.dot(jnp.concatenate(pieces, axis=0), own[at], preferred_element_type=F32)
        for pr, value in enumerate(join(out, 128)):
            ap[pr, at, :] = value

    eye = iota((128, 128), 0) == iota((128, 128), 1)

    def seek(req, hot, axis, swap):
        n = iota((1, 1024), 1)
        if swap:
            n = ((n >> 4) & 7) * 128 + (n >> 7) * R + (n & 15)

        def one(t, _):
            column = jnp.sum(jnp.where(eye, req[t], 0).astype(F32), axis=1, keepdims=True)[:ASKED].astype(I32)
            hot[t] = jnp.where(n == column, 1.0, 0.0).astype(BF16)
            return 0

        lax.fori_loop(0, LINE, one, 0)

    def serve(hot, t, store):
        got = jnp.dot(hot[t], store[...], preferred_element_type=F32).reshape(GROUPS, 8, 256)
        return jnp.concatenate([got[:, :, :128], got[:, :, 128:]], axis=1).astype(BF16)

    arrived(REQ_Y, "y", lambda s: req_y.at[s])
    arrived(REQ_Z, "z", lambda s: req_z.at[s])
    seek(req_y, hot_y, "y", True)
    seek(req_z, hot_z, "z", False)
    for role in range(2):
        landed(role)
    for d in (4, 3, 5, 2, 6, 1, 7):
        t = (y + d) % LINE
        pack_y[t] = serve(hot_y, t, store_y)
        op = copy(GHOST_Y, "y", t, pack_y.at[t], ghost.at[:, rows(y * 16, 16), :], y)
        op.start()
        started.append(op)
        t = (z + d) % LINE
        pack_z[t] = serve(hot_z, t, store_z)
        op = copy(GHOST_Z, "z", t, pack_z.at[t], ghost.at[:, rows(128 + z * 16, 16), :], z)
        op.start()
        started.append(op)
    ghost[:, rows(y * 16, 16), :] = serve(hot_y, y, store_y)
    ghost[:, rows(128 + z * 16, 16), :] = serve(hot_z, z, store_z)

    by_group = jnp.where(iota((16, 128), 1) >> 3 == iota((16, 128), 0), half_of, 0.0)
    by_slot = jnp.where((iota((128, 256), 0) & 7) == (iota((128, 256), 1) & 7), 1.0, 0.0)
    mask = jnp.dot(by_group.astype(BF16), by_slot.astype(BF16), preferred_element_type=F32)
    for b in range(GROUPS):
        upper = mask[b : b + 1]
        for h, m in ((0, 1.0 - upper), (1, upper)):
            for n in range(4):
                lhs[b, h * 256 + n * 64 : h * 256 + n * 64 + 64, :] = (
                    terms[n, b * 64 : b * 64 + 64, :] * m.astype(BF16)
                )
    arrived(PANEL, "c", lambda s: panel.at[s])
    arrived(PINDEX, "c", lambda s: idx_all.at[s])

    def make_wide(n, _):
        upper = idx_all[n]
        for h, m in ((0, 1.0 - upper), (1, upper)):
            for pr in range(2):
                wide[rows(n * 128 + h * 64, 64), pr * 512 : pr * 512 + 512] = (
                    panel[n, pr * 64 : pr * 64 + 64, :] * m.astype(BF16)
                )
        return 0

    lax.fori_loop(0, LINE, make_wide, 0)

    arrived(GHOST_Y, "y", lambda s: ghost.at[:, rows(s * 16, 16), :])
    arrived(GHOST_Z, "z", lambda s: ghost.at[:, rows(128 + s * 16, 16), :])

    for b in range(GROUPS):
        out = jnp.dot(lhs[b], ghost[b], preferred_element_type=F32)
        start = 8 * b // FAR * 32
        for pr, value in enumerate(join(out, 64)):
            ap[pr, start : start + 64, :] += value
    for pr in range(2):
        apb[pr * 512 : pr * 512 + 512] = ap[pr].astype(BF16)

    partial[...] = jnp.dot(wide[...], apb[...], preferred_element_type=F32).reshape(LINE, LINE, 2, 8, 128)
    for n in range(LINE):
        send_y[n] = partial[n, :, 0].reshape(64, 128).astype(BF16)
    push(SUM_Y, "y", lambda t: send_y.at[t], lambda s: sum_y.at[s])
    for n in range(LINE):
        send_z[n] = partial[:, n, 1].reshape(64, 128).astype(BF16)
    push(SUM_Z, "z", lambda t: send_z.at[t], lambda s: sum_z.at[s])
    arrived(SUM_Y, "y", lambda s: sum_y.at[s])
    acc = partial[y, :, 0].reshape(64, 128)
    for t in others("y"):
        acc = acc + sum_y[t].astype(F32)
    half_y[...] = acc.reshape(LINE, 8, 128)
    push(LAST_Y, "z", lambda t: half_y.at[t], lambda s: last_y.at[s])
    arrived(SUM_Z, "z", lambda s: sum_z.at[s])
    acc = partial[:, z, 1].reshape(64, 128)
    for t in others("z"):
        acc = acc + sum_z[t].astype(F32)
    half_z[...] = acc.reshape(LINE, 8, 128)
    push(LAST_Z, "y", lambda t: half_z.at[t], lambda s: last_z.at[s])
    arrived(LAST_Y, "z", lambda s: last_y.at[s])
    acc = half_y[z]
    for t in others("z"):
        acc = acc + last_y[t]
    out_ref[0:8] = acc
    arrived(LAST_Z, "y", lambda s: last_z.at[s])
    acc = half_z[y]
    for t in others("y"):
        acc = acc + last_z[t]
    out_ref[8:16] = acc
    for op in started:
        op.wait_send()


def shards(a_tiles, neighbors, send_rows, p_tiles, p_index):
    vmem = pl.BlockSpec(memory_space=pltpu.VMEM)
    V = pltpu.VMEM
    return pl.pallas_call(
        kernel,
        out_shape=jax.ShapeDtypeStruct((R, 128), F32),
        in_specs=[pl.BlockSpec(memory_space=pl.ANY)] * 5,
        out_specs=vmem,
        scratch_shapes=[
            V((K, R), I32), V((1, LINE * 64), I32), V((1, R), I32),
            V((K, R, 4096), BF16), V((R, 4096), BF16), V((LINE, 1, 256), I32),
            V((1024, 256), BF16), V((1024, 256), BF16),
            V((LINE, 1, 256), I32), V((LINE, LINE, 1, 256), I32), V((64, 256), I32),
            V((1, 128), I32), V((LINE, 1, 128), I32), V((LINE, 1, 128), I32),
            V((LINE, ASKED, 1024), BF16), V((LINE, ASKED, 1024), BF16),
            V((LINE, GROUPS, 16, 128), BF16), V((LINE, GROUPS, 16, 128), BF16),
            V((GROUPS, 256, 128), BF16),
            V((LINE, 128, 512), BF16), V((LINE, 1, 512), F32),
            V((512, 512), BF16), V((512, 1024), BF16), V((512, K * 128), BF16), V((512, 128), BF16),
            V((1024, 1024), BF16), V((GROUPS * 64, 1024), BF16), V((4, GROUPS * 64, 256), BF16),
            V((GROUPS, 512, 256), BF16), V((1024, 1024), BF16),
            V((512, 512), BF16), V((512, 512), BF16), V((512, 512), BF16),
            V((2, 512, 128), F32), V((1024, 128), BF16), V((LINE, LINE, 2, 8, 128), F32),
            V((LINE, 64, 128), BF16), V((LINE, 64, 128), BF16),
            V((LINE, 64, 128), BF16), V((LINE, 64, 128), BF16),
            V((LINE, 8, 128), F32), V((LINE, 8, 128), F32),
            V((LINE, 8, 128), F32), V((LINE, 8, 128), F32),
            pltpu.SemaphoreType.DMA((14, LINE)), pltpu.SemaphoreType.DMA((14, LINE)),
            pltpu.SemaphoreType.DMA((2, 12)), pltpu.SemaphoreType.DMA((2, 2, 2)), pltpu.SemaphoreType.DMA((2, 2, 2)),
            pltpu.SemaphoreType.DMA((2, 2)), pltpu.SemaphoreType.DMA((2, LINE)), pltpu.SemaphoreType.DMA((5,)),
        ],
        compiler_params=pltpu.CompilerParams(
            collective_id=0, has_side_effects=True, vmem_limit_bytes=56 * 2**20
        ),
    )(
        p_tiles.reshape(R, 4096),
        a_tiles.transpose(1, 0, 2),
        neighbors.T,
        send_rows,
        p_index.reshape(1, R),
    )


def solution(mesh):
    in_specs = (
        P("row", None, None),
        P("row", None),
        P("row", None),
        P("row", "col", None),
        P("row", "col"),
    )
    return jax.shard_map(shards, mesh=mesh, in_specs=in_specs, out_specs=P("row", "col"), check_vma=False)
```
